256 devices in a mesh: dp: 16 (over z, x_lo), tensor: 16 (over y, x_hi, core).
Axes of the slice: x: 4 (x_hi: 2, x_lo: 2; x = x_hi * 2 + x_lo), y: 4, z: 8, core: 2. Of those that a mesh axis runs over, the one named last changes fastest.
Arguments:
- gate_pre: bfloat16 [4096, 18432], P('dp', 'tensor'), may hold values from -6 to 6
- up_pre: bfloat16 [4096, 18432], P('dp', 'tensor'), may hold values from -6 to 6
- down_weight: bfloat16 [18432, 4608], P('tensor'), may hold values from -0.046875 to 0.046875
- out_grad: bfloat16 [4096, 4608], P(('dp', 'tensor')), may hold values from -24 to 24
Outputs:
- layer_out: bfloat16 [4096, 4608], P(('dp', 'tensor'))
- grad_gate: bfloat16 [4096, 18432], P('dp', 'tensor')
- grad_up: bfloat16 [4096, 18432], P('dp', 'tensor')
- grad_down: bfloat16 [18432, 4608], P('tensor', 'dp')
The draws below stay inside these ranges and needn't reach their ends.
All inputs are finite; a program needn't handle non-finite values.
Results may differ from the reference program's by a relative error of at most 0.023.
Values may be sent and summed in bfloat16 or wider, within the bound.
A program may use at most 128 MiB of HBM per device.

```python
import math
import jax
import jax.numpy as jnp
from jax import lax

D = 4608
HID = 18432
TOK_GRP = 256
TOKENS = 4096
N_DP = 16
N_TENSOR = 16


def with_spikes(entries, rng, source, target, parts, factor):
    def block_of(position):
        return (jnp.arange(entries.shape[position]) // (entries.shape[position] // parts)).reshape((-1,) + (1,) * (entries.ndim - 1 - position))

    one_side = jax.random.permutation(rng, parts)[block_of(target)]
    second = (block_of(target) + parts // 2) % parts
    return jnp.where((block_of(source) == one_side) | (block_of(source) == second), factor * entries, entries)


def block_scale(rng, shape, shards, low, top_value):
    def one(dim, parts):
        steps = jax.random.uniform(jax.random.fold_in(jax.random.fold_in(rng, 6), dim), (parts,), jnp.float32, low / len(shards), top_value / len(shards))
        return jnp.repeat(jnp.exp(steps), shape[dim] // parts).reshape((-1,) + (1,) * (len(shape) - dim - 1))

    factor_of = one(*shards[0])
    for cut in shards[1:]:
        factor_of = factor_of * one(*cut)
    return factor_of


def scatter_about(own_key, extent, spread, bound, cuts=(), held_as=jnp.bfloat16):
    entries = jax.random.normal(own_key, extent, jnp.float32) * spread
    if len(cuts) > 0:
        entries = block_scale(own_key, extent, cuts, -0.22, 0.18) * entries
    return jnp.clip(entries, min=-bound, max=bound).astype(held_as)


def bell_draw_with(stream_key, dims, width, reach, shards, heavy, kind=jnp.bfloat16):
    entries = width * jax.random.normal(stream_key, dims, jnp.float32)
    if shards:
        entries = entries * block_scale(stream_key, dims, shards, -0.22, 0.18)
    return jnp.clip(with_spikes(entries, jax.random.fold_in(stream_key, 3), *heavy), -reach, reach).astype(kind)


def setup_inputs(seed: int = 0) -> dict:
    arg_keys = jax.random.split(jax.random.key(seed), 5)
    gate_pre = scatter_about(arg_keys[0], (TOKENS, HID), 1.0, 6.0, ((0, 16), (1, 16)))
    up_pre = scatter_about(arg_keys[1], (TOKENS, HID), 1.0, 6.0, ((0, 16), (1, 16)))
    down_weight = scatter_about(arg_keys[2], (HID, D), HID ** -0.5, 0.046875, ((0, 16),))
    out_grad = bell_draw_with(arg_keys[3], (TOKENS, D), 1.0, 24.0, ((0, 256),), (0, 1, 256, 6.0))
    return {"gate_pre": gate_pre, "up_pre": up_pre, "down_weight": down_weight, "out_grad": out_grad}


def gelu_and_slope(value):
    coeff = math.sqrt(2.0 / math.pi)
    inner = coeff * (value + 0.044715 * value * value * value)
    tangent = jnp.tanh(inner)
    gelu = 0.5 * value * (1.0 + tangent)
    slope = 0.5 * (1.0 + tangent) + 0.5 * value * (1.0 - tangent * tangent) * coeff * (1.0 + 3.0 * 0.044715 * value * value)
    return (gelu, slope)

def reference(gate_pre, up_pre, down_weight, out_grad):
    gate_value = gate_pre.astype(jnp.float32)
    up_value = up_pre.astype(jnp.float32)
    gelu, slope = gelu_and_slope(gate_value)
    hidden = (gelu * up_value).astype(jnp.bfloat16)
    block_hid = HID // N_TENSOR

    def out_step(total, index):
        start = (index * block_hid).astype(jnp.int32)
        piece = lax.dynamic_slice_in_dim(hidden, start, block_hid, 1)
        rows = lax.dynamic_slice_in_dim(down_weight, start, block_hid, 0)
        part = jnp.dot(piece, rows, preferred_element_type=jnp.float32).astype(jnp.bfloat16)
        return (total + part.astype(jnp.float32), None)
    out_total, _ = lax.scan(out_step, jnp.zeros((hidden.shape[0], D), jnp.float32), jnp.arange(N_TENSOR, dtype=jnp.int32))
    layer_out = out_total.astype(jnp.bfloat16)
    grad_hidden = jnp.dot(out_grad, down_weight.T, preferred_element_type=jnp.float32)
    grad_gate = (grad_hidden * up_value * slope).astype(jnp.bfloat16)
    grad_up = (grad_hidden * gelu).astype(jnp.bfloat16)

    def down_step(total, index):
        start = (index * TOK_GRP).astype(jnp.int32)
        piece = lax.dynamic_slice_in_dim(hidden, start, TOK_GRP, 0)
        cots = lax.dynamic_slice_in_dim(out_grad, start, TOK_GRP, 0)
        part = jnp.dot(piece.T, cots, preferred_element_type=jnp.float32).astype(jnp.bfloat16)
        return (total + part.astype(jnp.float32), None)
    down_total, _ = lax.scan(down_step, jnp.zeros((HID, D), jnp.float32), jnp.arange(N_DP, dtype=jnp.int32))
    grad_down = down_total.astype(jnp.bfloat16)
    return (layer_out, grad_gate, grad_up, grad_down)
```

```python
import math

import jax
import jax.numpy as jnp
import numpy as np
from jax import lax
from jax.experimental import pallas as pl
from jax.experimental.pallas import tpu as pltpu
from jax.sharding import Mesh, PartitionSpec as P

BF = jnp.bfloat16
F32 = jnp.float32
AXES = ("z", "lo", "y", "hi", "core")
SIZES = dict(z=8, lo=2, y=4, hi=2, core=2)
D, HB, TOK, ROWS = 4608, 1152, 256, 16
COLS = 640
OUT_COLS = 288
WIDTHS = (256, 256, 256, 256, 128)
OFFSETS = tuple(sum(WIDTHS[:i]) for i in range(len(WIDTHS)))
Z_ORDER = (
    (0, 0), (1, 0), (0, 1), (1, 1), (0, 2), (1, 2), (2, 0), (0, 3), (1, 3),
    (3, 0), (2, 1), (4, 0), (3, 1), (2, 2), (4, 1), (3, 2), (2, 3), (4, 2), (3, 3), (4, 3),
)
WT = 512
COEFF = math.sqrt(2.0 / math.pi)


def gelu_and_slope(value):
    square = value * value
    tangent = jnp.tanh(COEFF * value * (1.0 + 0.044715 * square))
    gelu = 0.5 * value * (1.0 + tangent)
    slope = 0.5 * (1.0 + tangent) + 0.5 * value * (1.0 - tangent * tangent) * COEFF * (
        1.0 + 3.0 * 0.044715 * square
    )
    return gelu, slope


def z_plan():
    link, arrived, issue, done = 4.0, {}, {}, {}
    for chunk, hop in Z_ORDER:
        ready = 0.3 * chunk if hop == 0 else arrived[chunk, hop - 1]
        start = max(link, ready)
        link = start + 2.65 * WIDTHS[chunk] / 256 * (0.5 if hop == 3 else 1.0)
        arrived[chunk, hop] = link + 2.0
        issue[chunk, hop] = max(start - 3.0, ready)
        if hop == 3:
            done[chunk] = link + 2.0
    return issue, done


def kernel(
    gate, up, w, og, lout, ggrad, ugrad, dgrad,
    gv, uv, wv, hall, ogall, ogc, ogct, part, crecv, ysum, yhalf, yblk, hsend, hrecv, lov,
    gelu_s, us_s, ggv, guv, losend, lorecv, own, gdv, sems,
):
    idx = {a: lax.axis_index(a) for a in AXES}
    z, lo, y, hi, c = (idx[a] for a in AXES)
    count = [0]

    def sem():
        count[0] += 1
        return sems.at[count[0] - 1]

    def shifted(axis, delta):
        return lax.rem(idx[axis] + (delta % SIZES[axis]), SIZES[axis])

    def at(axis, delta):
        return {axis: shifted(axis, delta)}

    def local(src, dst):
        return pltpu.make_async_copy(src, dst, sem())

    sent = []

    def remote(src, dst, axis, delta):
        return pltpu.make_async_remote_copy(
            src_ref=src, dst_ref=dst, send_sem=sem(), recv_sem=sem(),
            device_id=at(axis, delta), device_id_type=pl.DeviceIdType.MESH,
        )

    def go(copy):
        copy.start()
        sent.append(copy)

    peers = [("z", d) for d in range(1, 8)] + [("lo", 1), ("y", 1), ("y", 3), ("hi", 1), ("core", 1)]
    barrier = pltpu.get_barrier_semaphore()
    for axis, delta in peers:
        pl.semaphore_signal(
            barrier, inc=1, device_id=at(axis, delta), device_id_type=pl.DeviceIdType.MESH
        )

    def chunk_cols(k):
        return pl.ds(OFFSETS[k], WIDTHS[k])

    loads = []
    for k in range(len(WIDTHS)):
        pair = (
            local(gate.at[:, chunk_cols(k)], gv.at[:, chunk_cols(k)]),
            local(up.at[:, chunk_cols(k)], uv.at[:, chunk_cols(k)]),
        )
        loads.append(pair)

    def window(zt):
        return pl.ds(pl.multiple_of(lax.div(zt * 9, 2) * 128, 128), COLS)

    load_og = local(og, ogall.at[y, hi, c])
    load_ogc = local(og.at[:, window(z)], ogc.at[y, hi, c, 0])
    load_w = [
        local(w.at[:, pl.ds(j * WT, WT)], wv.at[:, pl.ds(j * WT, WT)]) for j in range(D // WT)
    ]
    for pair in loads[:1]:
        pair[0].start()
        pair[1].start()
    load_og.start()
    load_ogc.start()
    for pair in loads[1:]:
        pair[0].start()
        pair[1].start()
    for copy in load_w:
        copy.start()

    def hidden(k):
        loads[k][0].wait()
        loads[k][1].wait()
        cols = chunk_cols(k)
        up_value = uv[:, cols].astype(F32)
        gelu, slope = gelu_and_slope(gv[:, cols].astype(F32))
        hall[pl.ds(0, TOK), cols] = (gelu * up_value).astype(BF)
        gelu_s[:, cols] = gelu
        us_s[:, cols] = up_value * slope

    steps = []

    def add(when, run):
        steps.append((when, len(steps), run))

    hidden(0)
    pl.semaphore_wait(barrier, len(peers))

    a2a = [
        remote(og.at[:, window(shifted("z", d))], ogc.at[y, hi, c, d], "z", d) for d in range(1, 8)
    ]

    class Gather:
        def __init__(self, buf):
            def move(yd, hd, axis, delta):
                ref = buf.at[shifted("y", yd), shifted("hi", hd), c]
                return remote(ref, ref, axis, delta)

            self.hi = move(0, 0, "hi", 1)
            self.right = [move(0, 0, "y", 1), move(0, 1, "y", 1), move(3, 0, "y", 1)]
            self.left = [move(0, 0, "y", 3), move(0, 1, "y", 3), move(1, 1, "y", 3)]
            self.core = {(yd, hd): move(yd, hd, "core", 1) for yd in range(4) for hd in range(2)}

        def schedule(self, t, first):
            def begin():
                first()
                go(self.right[0])
                go(self.left[0])
                go(self.hi)
                go(self.core[0, 0])

            def got_hi():
                self.hi.wait_recv()
                go(self.right[1])
                go(self.left[1])
                go(self.core[0, 1])

            def got_first():
                self.right[0].wait_recv()
                go(self.right[2])
                go(self.core[3, 0])
                self.left[0].wait_recv()
                go(self.core[1, 0])

            def got_second():
                self.left[1].wait_recv()
                go(self.left[2])
                go(self.core[1, 1])
                self.right[1].wait_recv()
                go(self.core[3, 1])

            def got_far():
                self.right[2].wait_recv()
                go(self.core[2, 0])
                self.left[2].wait_recv()
                go(self.core[2, 1])

            def finish():
                for copy in self.core.values():
                    copy.wait_recv()

            for when, run in zip(t, (begin, got_hi, got_first, got_second, got_far, finish)):
                add(when, run)

    rows = Gather(ogall)
    columns = Gather(ogc)

    def start_rows():
        load_og.wait()

    def start_columns():
        load_ogc.wait()
        for copy in a2a:
            copy.wait_recv()

    rows.schedule((0.01, 5.0, 5.5, 10.0, 15.0, 16.5), start_rows)
    columns.schedule((9.0, 14.0, 14.5, 19.0, 24.0, 25.5), start_columns)
    add(0.0, lambda: [go(copy) for copy in a2a])

    hops = {}
    for k in range(len(WIDTHS)):
        cols = chunk_cols(k)
        for hop in range(4):
            first, size = 256 * hop, 256
            if hop == 3:
                size = 128
            hops[k, hop, 0] = remote(
                hall.at[pl.ds(first, size), cols], hall.at[pl.ds(first + 256, size), cols], "z", 1
            )
            first = 0 if hop == 0 else 256 * (8 - hop)
            into = 256 * (7 - hop)
            if hop == 3:
                first, into = first + 128, into + 128
            hops[k, hop, 1] = remote(
                hall.at[pl.ds(first, size), cols], hall.at[pl.ds(into, size), cols], "z", 7
            )
    issue, done = z_plan()

    def z_step(k, hop):
        for way in range(2):
            if hop > 0:
                hops[k, hop - 1, way].wait_recv()
            go(hops[k, hop, way])

    for k, hop in Z_ORDER:
        add(issue[k, hop] + 0.02, lambda k=k, hop=hop: z_step(k, hop))
    for k in range(1, len(WIDTHS)):
        add(0.01 + 0.3 * (k - 1), lambda k=k: hidden(k))

    def forward(j):
        load_w[j].wait()
        cols = pl.ds(j * WT, WT)
        out = jnp.dot(hall[pl.ds(0, TOK), :], wv[:, cols], preferred_element_type=F32)
        part[:, :, :, :, cols] = out.astype(BF).reshape(4, 2, 2, ROWS, WT)

    for j in range(D // WT):
        add(1.8 + 0.5 * j, lambda j=j: forward(j))

    core_send = {}
    for yd in (2, 1, 3, 0):
        yy = shifted("y", yd)
        core_send[yd] = remote(part.at[yy, :, 1 - c], crecv.at[yy], "core", 1)
    y2 = shifted("y", 2)
    half_send = [
        remote(ysum.at[y2, 0], yhalf.at[0], "y", 1),
        remote(ysum.at[y2, 1], yhalf.at[1], "y", 3),
    ]
    blk_send = [
        remote(ysum.at[shifted("y", 1)], yblk.at[0], "y", 1),
        remote(ysum.at[shifted("y", 3)], yblk.at[1], "y", 3),
    ]
    hi_send = remote(hsend, hrecv, "hi", 1)
    store_lout = local(lov, lout)

    def scatter_core():
        for yd in (2, 1, 3, 0):
            go(core_send[yd])

    def scatter_far():
        core_send[2].wait_recv()
        ysum[y2] = (part[y2, :, c].astype(F32) + crecv[y2].astype(F32)).astype(BF)
        go(half_send[0])
        go(half_send[1])

    def scatter_near():
        for way in range(2):
            yd = 1 if way == 0 else 3
            yy = shifted("y", yd)
            core_send[yd].wait_recv()
            half_send[way].wait_recv()
            plain = 1 - way
            ysum[yy, plain] = (part[yy, plain, c].astype(F32) + crecv[yy, plain].astype(F32)).astype(BF)
            ysum[yy, way] = (
                part[yy, way, c].astype(F32) + crecv[yy, way].astype(F32) + yhalf[way].astype(F32)
            ).astype(BF)
            go(blk_send[way])

    def mine(hh):
        total = part[y, hh, c].astype(F32) + crecv[y, hh].astype(F32)
        return total + yblk[0, hh].astype(F32) + yblk[1, hh].astype(F32)

    def scatter_hi():
        core_send[0].wait_recv()
        blk_send[0].wait_recv()
        blk_send[1].wait_recv()
        hsend[...] = mine(1 - hi).astype(BF)
        go(hi_send)

    def scatter_end():
        hi_send.wait_recv()
        lov[...] = (mine(hi) + hrecv[...].astype(F32)).astype(BF)
        store_lout.start()

    add(7.5, scatter_core)
    add(10.5, scatter_far)
    add(15.5, scatter_near)
    add(24.0, scatter_hi)
    add(29.0, scatter_end)

    stores = []

    def backward(k):
        cols = chunk_cols(k)
        group = ogall[...].reshape(TOK, D)
        grad = lax.dot_general(
            group, wv[cols, :], (((1,), (1,)), ((), ())), preferred_element_type=F32
        )
        ggv[:, cols] = (grad * us_s[:, cols]).astype(BF)
        guv[:, cols] = (grad * gelu_s[:, cols]).astype(BF)
        for src, dst in ((ggv, ggrad), (guv, ugrad)):
            copy = local(src.at[:, cols], dst.at[:, cols])
            copy.start()
            stores.append(copy)

    for k in range(len(WIDTHS)):
        add(16.6 + 0.8 * k, lambda k=k: backward(k))

    def transpose(s):
        block = ogc[:, :, :, s].reshape(TOK, COLS)
        ogct[:, pl.ds(TOK * s, TOK)] = block.T

    for s in range(8):
        add(25.6 + 0.2 * s, lambda s=s: transpose(s))

    first_row = pl.multiple_of(64 * lax.rem(z, 2), 64)
    lo_send = [
        remote(losend.at[:, chunk_cols(k)], lorecv.at[:, chunk_cols(k)], "lo", 1)
        for k in range(len(WIDTHS))
    ]

    def weight_grad(k):
        cols = chunk_cols(k)
        for way in range(2):
            hops[k, 3, way].wait_recv()
        total = jnp.dot(
            ogct[pl.ds(first_row, 2 * OUT_COLS), :], hall[:, cols], preferred_element_type=F32
        )
        low, high = total[:OUT_COLS], total[OUT_COLS:]
        losend[:, cols] = jnp.where(lo == 0, high, low).astype(BF)
        go(lo_send[k])
        own[:, cols] = jnp.where(lo == 0, low, high)

    def weight_end(k):
        cols = chunk_cols(k)
        lo_send[k].wait_recv()
        total = own[:, cols] + lorecv[:, cols].astype(F32)
        total = jnp.concatenate([total, jnp.zeros((96, WIDTHS[k]), F32)], axis=0)
        gdv[cols, :] = total.T[:, :OUT_COLS].astype(BF)
        copy = local(gdv.at[cols], dgrad.at[cols])
        copy.start()
        stores.append(copy)

    free = 27.3
    for k in range(len(WIDTHS)):
        free = max(free, done[k]) + 0.05
        add(free, lambda k=k: weight_grad(k))
        free += 0.4
    prev = 0.0
    for k in range(len(WIDTHS)):
        prev = max(prev, max(27.3, done[k])) + 5.5 * WIDTHS[k] / 256
        add(prev, lambda k=k: weight_end(k))

    for _, _, run in sorted(steps, key=lambda item: item[:2]):
        run()
    for copy in sent:
        copy.wait_send()
    store_lout.wait()
    for copy in stores:
        copy.wait()


def body(gate, up, w, og):
    any_spec = pl.BlockSpec(memory_space=pl.ANY)
    shapes = (
        jax.ShapeDtypeStruct((ROWS, D), BF),
        jax.ShapeDtypeStruct((TOK, HB), BF),
        jax.ShapeDtypeStruct((TOK, HB), BF),
        jax.ShapeDtypeStruct((HB, OUT_COLS), BF),
    )
    v = pltpu.VMEM
    scratch = [
        v((TOK, HB), BF), v((TOK, HB), BF), v((HB, D), BF),
        v((8 * TOK, HB), BF), v((4, 2, 2, ROWS, D), BF), v((4, 2, 2, 8, ROWS, COLS), BF),
        v((COLS, 8 * TOK), BF),
        v((4, 2, 2, ROWS, D), BF), v((4, 2, ROWS, D), BF), v((4, 2, ROWS, D), BF),
        v((2, ROWS, D), BF), v((2, 2, ROWS, D), BF), v((ROWS, D), BF), v((ROWS, D), BF), v((ROWS, D), BF),
        v((TOK, HB), F32), v((TOK, HB), F32), v((TOK, HB), BF), v((TOK, HB), BF),
        v((OUT_COLS, HB), BF), v((OUT_COLS, HB), BF), v((OUT_COLS, HB), F32), v((HB, OUT_COLS), BF),
        pltpu.SemaphoreType.DMA((256,)),
    ]
    return pl.pallas_call(
        kernel,
        out_shape=shapes,
        in_specs=[any_spec] * 4,
        out_specs=(any_spec,) * 4,
        scratch_shapes=scratch,
        compiler_params=pltpu.CompilerParams(
            collective_id=0, has_side_effects=True, vmem_limit_bytes=60 * 2**20
        ),
        cost_estimate=pl.CostEstimate(
            flops=6 * TOK * HB * D, bytes_accessed=14_000_000, transcendentals=TOK * HB
        ),
        name="geglu_down",
    )(gate, up, w, og)


def solution(mesh):
    fine = Mesh(mesh.devices.reshape(tuple(SIZES[a] for a in AXES)), AXES)
    dp, tensor = ("z", "lo"), ("y", "hi", "core")
    return jax.shard_map(
        body,
        mesh=fine,
        in_specs=(P(dp, tensor), P(dp, tensor), P(tensor, None), P(dp + tensor, None)),
        out_specs=(P(dp + tensor, None), P(dp, tensor), P(dp, tensor), P(tensor, dp)),
        check_vma=False,
    )
```

```python
import math

import jax
import jax.numpy as jnp
from jax import lax
from jax.experimental import pallas as pl
from jax.experimental.pallas import tpu as pltpu
from jax.sharding import Mesh, PartitionSpec as P

BF = jnp.bfloat16
F32 = jnp.float32
AXES = ("z", "lo", "y", "hi", "core")
SIZES = dict(z=8, lo=2, y=4, hi=2, core=2)
D, HB, TOK, ROWS = 4608, 1152, 256, 16
COLS = 640
OUT_COLS = 288
WIDTHS = (384, 384, 128, 128, 128)
OFFSETS = tuple(sum(WIDTHS[:i]) for i in range(len(WIDTHS)))
Z_ORDER = (
    (0, 0), (1, 0), (0, 1), (1, 1), (0, 2), (1, 2), (0, 3), (2, 0), (1, 3), (3, 0),
    (2, 1), (4, 0), (3, 1), (2, 2), (4, 1), (3, 2), (2, 3), (4, 2), (3, 3), (4, 3),
)
WT = 512
COEFF = math.sqrt(2.0 / math.pi)


def gelu_and_slope(value):
    square = value * value
    tangent = jnp.tanh(COEFF * value * (1.0 + 0.044715 * square))
    gelu = 0.5 * value * (1.0 + tangent)
    slope = 0.5 * (1.0 + tangent) + 0.5 * value * (1.0 - tangent * tangent) * COEFF * (
        1.0 + 3.0 * 0.044715 * square
    )
    return gelu, slope


LANES = dict(z=(20.2, 2.0), y=(20.2, 2.6), x=(20.2, 2.6), core=(4.0, 2.0))


class Move:
    def __init__(self, copy, lane, src, hops=1):
        self.dma, self.lane, self.landed = copy, lane, None
        rate, self.lag = LANES[lane.rstrip("+-")]
        self.busy = rate * math.prod(src.shape) * 2e-6 * hops
        self.lag += 0.6 * (hops - 1)


class Steps:
    def __init__(self):
        self.items = {}

    def add(self, key, rank, act=None, waits=(), starts=(), after=(), cost=0.0):
        self.items[key] = (rank, act, tuple(waits), tuple(starts), tuple(after), cost)

    def order(self):
        now, idle, left, done, out = 0.0, {}, dict(self.items), set(), []
        while left:
            best = None
            for key, (rank, _, waits, _, after, _) in left.items():
                if any(k not in done for k in after) or any(m.landed is None for m in waits):
                    continue
                ready = max([now] + [m.landed for m in waits])
                choice = (ready, rank, key)
                if best is None or choice[:2] < best[:2]:
                    best = choice
            ready, _, key = best
            _, _, _, starts, _, cost = left.pop(key)
            now = ready + cost
            for move in starts:
                now += 0.05
                begin = max(now, idle.get(move.lane, 0.0))
                idle[move.lane] = begin + move.busy
                move.landed = idle[move.lane] + move.lag
            done.add(key)
            out.append((ready, now, key))
        return out

    def emit(self):
        sent = []
        for _, _, key in self.order():
            _, act, waits, starts, _, _ = self.items[key]
            for move in waits:
                move.dma.wait_recv()
            if act is not None:
                act()
            for move in starts:
                move.dma.start()
                sent.append(move)
        for move in sent:
            move.dma.wait_send()


def kernel(
    gate, up, w, og, lout, ggrad, ugrad, dgrad,
    gv, uv, wv, hall, ogall, ogc, ogct, part, crecv, ysum, yhalf, yblk, hsend, hrecv, lov,
    gelu_s, us_s, ggv, guv, acc, losend, lorecv, own, gdv, sems,
):
    idx = {a: lax.axis_index(a) for a in AXES}
    z, lo, y, hi, c = (idx[a] for a in AXES)
    count = [0]

    def sem():
        count[0] += 1
        return sems.at[count[0] - 1]

    def shifted(axis, delta):
        return lax.rem(idx[axis] + (delta % SIZES[axis]), SIZES[axis])

    def at(axis, delta):
        return {axis: shifted(axis, delta)}

    def local(src, dst):
        return pltpu.make_async_copy(src, dst, sem())

    def remote(src, dst, axis, delta):
        copy = pltpu.make_async_remote_copy(
            src_ref=src, dst_ref=dst, send_sem=sem(), recv_sem=sem(),
            device_id=at(axis, delta), device_id_type=pl.DeviceIdType.MESH,
        )
        lane, hops = axis, 1
        if axis in ("hi", "lo"):
            lane = "x"
        elif axis in ("z", "y"):
            hops = min(delta, SIZES[axis] - delta)
            lane = axis + ("+" if delta == hops else "-")
        return Move(copy, lane, src, hops)

    peers = [("z", d) for d in range(1, 8)] + [("lo", 1), ("y", 1), ("y", 3), ("hi", 1), ("core", 1)]
    barrier = pltpu.get_barrier_semaphore()
    for axis, delta in peers:
        pl.semaphore_signal(
            barrier, inc=1, device_id=at(axis, delta), device_id_type=pl.DeviceIdType.MESH
        )

    def chunk_cols(k):
        return pl.ds(OFFSETS[k], WIDTHS[k])

    loads = []
    for k in range(len(WIDTHS)):
        pair = (
            local(gate.at[:, chunk_cols(k)], gv.at[:, chunk_cols(k)]),
            local(up.at[:, chunk_cols(k)], uv.at[:, chunk_cols(k)]),
        )
        loads.append(pair)

    def window(zt):
        return pl.ds(pl.multiple_of(lax.div(zt * 9, 2) * 128, 128), COLS)

    load_og = local(og, ogall.at[y, hi, c])
    load_ogc = local(og.at[:, window(z)], ogc.at[y, hi, c, 0])
    load_w = [
        local(w.at[:, pl.ds(j * WT, WT)], wv.at[:, pl.ds(j * WT, WT)]) for j in range(D // WT)
    ]
    for pair in loads[:1]:
        pair[0].start()
        pair[1].start()
    load_og.start()
    load_ogc.start()
    for pair in loads[1:]:
        pair[0].start()
        pair[1].start()
    for copy in load_w:
        copy.start()

    def hidden(k):
        loads[k][0].wait()
        loads[k][1].wait()
        cols = chunk_cols(k)
        up_value = uv[:, cols].astype(F32)
        gelu, slope = gelu_and_slope(gv[:, cols].astype(F32))
        hall[pl.ds(0, TOK), cols] = (gelu * up_value).astype(BF)
        gelu_s[:, cols] = gelu
        us_s[:, cols] = up_value * slope

    steps = Steps()
    add = steps.add
    chunks = range(len(WIDTHS))
    hidden(0)
    hidden(1)
    pl.semaphore_wait(barrier, len(peers))

    a2a = [
        remote(og.at[:, window(shifted("z", d))], ogc.at[y, hi, c, d], "z", d) for d in range(1, 8)
    ]
    add("columns out", 0, starts=a2a)

    def gather(name, buf, rank, act, waits, after, later):
        def move(yd, hd, axis, delta):
            ref = buf.at[shifted("y", yd), shifted("hi", hd), c]
            return remote(ref, ref, axis, delta)

        across = move(0, 0, "hi", 1)
        right = [move(0, 0, "y", 1), move(0, 1, "y", 1), move(3, 0, "y", 1)]
        left = [move(0, 0, "y", 3), move(0, 1, "y", 3), move(1, 1, "y", 3)]
        core = {(yd, hd): move(yd, hd, "core", 1) for yd in range(4) for hd in range(2)}

        def part(i, wait, *starts):
            add((name, i), rank, waits=(wait,), starts=starts, after=later.get(i, ()))

        add((name, 0), rank, act, waits, (right[0], left[0], across, core[0, 0]), after)
        part(1, across, right[1], left[1], core[0, 1])
        part(2, right[0], right[2], core[3, 0])
        part(3, left[0], core[1, 0])
        part(4, left[1], left[2], core[1, 1])
        part(5, right[1], core[3, 1])
        part(6, right[2], core[2, 0])
        part(7, left[2], core[2, 1])
        add((name, 8), rank, waits=core.values(), after=[(name, i) for i in range(8)])

    first_columns = {i: [("columns", 2), ("columns", 4)] for i in (2, 4)}
    gather("rows", ogall, 3, load_og.wait, (), ("columns out",), first_columns)
    gather("columns", ogc, 2, load_ogc.wait, a2a, (), {})

    hops = {}
    for k in chunks:
        cols = chunk_cols(k)
        for hop in range(4):
            first, size = 256 * hop, 256
            if hop == 3:
                size = 128
            hops[k, hop, 0] = remote(
                hall.at[pl.ds(first, size), cols], hall.at[pl.ds(first + 256, size), cols], "z", 1
            )
            first = 0 if hop == 0 else 256 * (8 - hop)
            into = 256 * (7 - hop)
            if hop == 3:
                first, into = first + 128, into + 128
            hops[k, hop, 1] = remote(
                hall.at[pl.ds(first, size), cols], hall.at[pl.ds(into, size), cols], "z", 7
            )
    for i, (k, hop) in enumerate(Z_ORDER):
        for way in range(2):
            after = [("z", *Z_ORDER[i - 1], way)] if i else ["columns out"]
            if hop == 0 and k > 1:
                after.append(("hidden", k))
            waits = (hops[k, hop - 1, way],) if hop else ()
            add(("z", k, hop, way), 1, waits=waits, starts=(hops[k, hop, way],), after=after)
    for k in chunks[2:]:
        add(("hidden", k), 4, lambda k=k: hidden(k), after=[("rows", 0)], cost=0.9 * WIDTHS[k] / 256)

    def forward(j):
        load_w[j].wait()
        cols = pl.ds(j * WT, WT)
        out = jnp.dot(hall[pl.ds(0, TOK), :], wv[:, cols], preferred_element_type=F32)
        part[:, :, :, :, cols] = out.astype(BF).reshape(4, 2, 2, ROWS, WT)

    tiles = range(D // WT)
    for j in tiles:
        add(("forward", j), 5, lambda j=j: forward(j), after=[("hidden", k) for k in chunks[2:]], cost=0.6)

    core_send = {}
    for yd in (2, 1, 3, 0):
        yy = shifted("y", yd)
        core_send[yd] = remote(part.at[yy, :, 1 - c], crecv.at[yy], "core", 1)
    y2 = shifted("y", 2)
    half_send = [
        remote(ysum.at[y2, 0], yhalf.at[0], "y", 1),
        remote(ysum.at[y2, 1], yhalf.at[1], "y", 3),
    ]
    blk_send = [
        remote(ysum.at[shifted("y", 1)], yblk.at[0], "y", 1),
        remote(ysum.at[shifted("y", 3)], yblk.at[1], "y", 3),
    ]
    hi_send = remote(hsend, hrecv, "hi", 1)
    store_lout = local(lov, lout)

    def scatter_far():
        ysum[y2] = (part[y2, :, c].astype(F32) + crecv[y2].astype(F32)).astype(BF)

    def scatter_near(way):
        yy = shifted("y", 1 if way == 0 else 3)
        plain = 1 - way
        ysum[yy, plain] = (part[yy, plain, c].astype(F32) + crecv[yy, plain].astype(F32)).astype(BF)
        ysum[yy, way] = (
            part[yy, way, c].astype(F32) + crecv[yy, way].astype(F32) + yhalf[way].astype(F32)
        ).astype(BF)

    def mine(hh):
        total = part[y, hh, c].astype(F32) + crecv[y, hh].astype(F32)
        return total + yblk[0, hh].astype(F32) + yblk[1, hh].astype(F32)

    def scatter_hi():
        hsend[...] = mine(1 - hi).astype(BF)

    def scatter_end():
        lov[...] = (mine(hi) + hrecv[...].astype(F32)).astype(BF)
        store_lout.start()

    add("scatter core", 3, starts=core_send.values(), after=[("forward", j) for j in tiles])
    add("scatter far", 3, scatter_far, (core_send[2],), half_send, cost=0.3)
    for way in range(2):
        waits = (core_send[1 + 2 * way], half_send[way])
        add(("near", way), 3, lambda way=way: scatter_near(way), waits, (blk_send[way],), [("rows", 2), ("rows", 4)], cost=0.3)
    add("scatter hi", 3, scatter_hi, (core_send[0], *blk_send), (hi_send,), cost=0.2)
    add("scatter end", 3, scatter_end, (hi_send,), cost=0.2)

    stores = []

    def backward(k):
        cols = chunk_cols(k)
        group = ogall[...].reshape(TOK, D)
        grad = lax.dot_general(
            group, wv[cols, :], (((1,), (1,)), ((), ())), preferred_element_type=F32
        )
        ggv[:, cols] = (grad * us_s[:, cols]).astype(BF)
        guv[:, cols] = (grad * gelu_s[:, cols]).astype(BF)
        for src, dst in ((ggv, ggrad), (guv, ugrad)):
            copy = local(src.at[:, cols], dst.at[:, cols])
            copy.start()
            stores.append(copy)

    for k in chunks:
        add(("backward", k), 6, lambda k=k: backward(k), after=[("rows", 8)], cost=1.1 * WIDTHS[k] / 256)

    def transpose(s):
        block = ogc[:, :, :, s].reshape(TOK, COLS)
        ogct[:, pl.ds(TOK * s, TOK)] = block.T

    for s in range(8):
        add(("transpose", s), 2, lambda s=s: transpose(s), after=[("columns", 8)], cost=0.25)

    first_row = pl.multiple_of(64 * lax.rem(z, 2), 64)
    window_rows = pl.ds(first_row, 2 * OUT_COLS)
    lo_send = [
        remote(losend.at[:, chunk_cols(k)], lorecv.at[:, chunk_cols(k)], "lo", 1) for k in chunks
    ]

    def product(k, first, size):
        return jnp.dot(
            ogct[window_rows, pl.ds(first, size)], hall[pl.ds(first, size), chunk_cols(k)],
            preferred_element_type=F32,
        )

    def weight_most(k):
        acc[:, chunk_cols(k)] = product(k, 0, 1024) + product(k, 1280, 768)

    def weight_last(k):
        cols = chunk_cols(k)
        total = acc[:, cols] + product(k, 1024, 256)
        low, high = total[:OUT_COLS], total[OUT_COLS:]
        losend[:, cols] = jnp.where(lo == 0, high, low).astype(BF)
        own[:, cols] = jnp.where(lo == 0, low, high)

    def weight_end(k):
        cols = chunk_cols(k)
        gdv[:, cols] = (own[:, cols] + lorecv[:, cols].astype(F32)).astype(BF)
        copy = local(gdv.at[:, cols], dgrad.at[:, cols])
        copy.start()
        stores.append(copy)

    transposed = [("transpose", s) for s in range(8)]
    for k in chunks:
        after = transposed + [("z", k, 3, 0), ("z", k, 3, 1)]
        size = (WIDTHS[k] + 255) // 256
        add(("most", k), 2, lambda k=k: weight_most(k), after=after, cost=0.75 * size)
        add(
            ("last", k), 1, lambda k=k: weight_last(k), (hops[k, 3, 0], hops[k, 3, 1]),
            (lo_send[k],), [("most", k)], 0.3 * size,
        )
        add(("end", k), 3, lambda k=k: weight_end(k), (lo_send[k],), cost=0.2 * size)

    steps.emit()
    store_lout.wait()
    for copy in stores:
        copy.wait()


def body(gate, up, w, og):
    any_spec = pl.BlockSpec(memory_space=pl.ANY)
    shapes = (
        jax.ShapeDtypeStruct((ROWS, D), BF),
        jax.ShapeDtypeStruct((TOK, HB), BF),
        jax.ShapeDtypeStruct((TOK, HB), BF),
        jax.ShapeDtypeStruct((OUT_COLS, HB), BF),
    )
    v = pltpu.VMEM
    scratch = [
        v((TOK, HB), BF), v((TOK, HB), BF), v((HB, D), BF),
        v((8 * TOK, HB), BF), v((4, 2, 2, ROWS, D), BF), v((4, 2, 2, 8, ROWS, COLS), BF),
        v((COLS, 8 * TOK), BF),
        v((4, 2, 2, ROWS, D), BF), v((4, 2, ROWS, D), BF), v((4, 2, ROWS, D), BF),
        v((2, ROWS, D), BF), v((2, 2, ROWS, D), BF), v((ROWS, D), BF), v((ROWS, D), BF), v((ROWS, D), BF),
        v((TOK, HB), F32), v((TOK, HB), F32), v((TOK, HB), BF), v((TOK, HB), BF),
        v((2 * OUT_COLS, HB), F32),
        v((OUT_COLS, HB), BF), v((OUT_COLS, HB), BF), v((OUT_COLS, HB), F32), v((OUT_COLS, HB), BF),
        pltpu.SemaphoreType.DMA((256,)),
    ]
    results = pl.pallas_call(
        kernel,
        out_shape=shapes,
        in_specs=[any_spec] * 4,
        out_specs=(any_spec,) * 4,
        scratch_shapes=scratch,
        compiler_params=pltpu.CompilerParams(
            collective_id=0, has_side_effects=True, vmem_limit_bytes=60 * 2**20
        ),
        cost_estimate=pl.CostEstimate(
            flops=6 * TOK * HB * D, bytes_accessed=14_000_000, transcendentals=TOK * HB
        ),
        name="geglu_down",
    )(gate, up, w, og)
    layer_out, grad_gate, grad_up, grad_down = finish(results)
    return layer_out, grad_gate, grad_up, grad_down.T


def finish_kernel(*refs):
    n = len(refs) // 3
    sources, targets, held = refs[:n], refs[n : 2 * n], refs[2 * n : 3 * n]
    sems = refs[3 * n]
    moves = []
    for source, target, mid in zip(sources, targets, held):
        rows = source.shape[0]
        pieces = 1 if rows < 128 else 4 if rows % 64 == 0 else 3
        for piece in range(pieces):
            part = pl.ds(piece * (rows // pieces), rows // pieces)
            k = len(moves)
            moves.append(
                (
                    pltpu.make_async_copy(source.at[part], mid.at[part], sems.at[0, k]),
                    pltpu.make_async_copy(mid.at[part], target.at[part], sems.at[1, k]),
                )
            )
    for first, _ in moves:
        first.start()
    for first, second in moves:
        first.wait()
        second.start()
    for _, second in moves:
        second.wait()


def finish(results):
    any_spec = pl.BlockSpec(memory_space=pl.ANY)
    n = len(results)
    return pl.pallas_call(
        finish_kernel,
        out_shape=tuple(jax.ShapeDtypeStruct(r.shape, r.dtype) for r in results),
        in_specs=[any_spec] * n,
        out_specs=(any_spec,) * n,
        scratch_shapes=[pltpu.VMEM(r.shape, r.dtype) for r in results]
        + [pltpu.SemaphoreType.DMA((2, 4 * n))],
        compiler_params=pltpu.CompilerParams(vmem_limit_bytes=60 * 2**20),
        name="finish",
    )(*results)


def solution(mesh):
    fine = Mesh(mesh.devices.reshape(tuple(SIZES[a] for a in AXES)), AXES)
    dp, tensor = ("z", "lo"), ("y", "hi", "core")
    return jax.shard_map(
        body,
        mesh=fine,
        in_specs=(P(dp, tensor), P(dp, tensor), P(tensor, None), P(dp + tensor, None)),
        out_specs=(P(dp + tensor, None), P(dp, tensor), P(dp, tensor), P(tensor, dp)),
        check_vma=False,
    )
```

```python
import math

import jax
import jax.numpy as jnp
from jax import lax
from jax.experimental import pallas as pl
from jax.experimental.pallas import tpu as pltpu
from jax.sharding import Mesh, PartitionSpec as P

BF = jnp.bfloat16
F32 = jnp.float32
AXES = ("z", "lo", "y", "hi", "core")
SIZES = dict(z=8, lo=2, y=4, hi=2, core=2)
D, HB, TOK, ROWS = 4608, 1152, 256, 16
COLS = 640
OUT_COLS = 288
WIDTHS = (256, 256, 256, 128, 128, 128)
OFFSETS = tuple(sum(WIDTHS[:i]) for i in range(len(WIDTHS)))
Z_ORDER = ((3, 0), (2, 0), (1, 0), (0, 0), (2, 1), (0, 1), (1, 1), (5, 0), (4, 0), (2, 2), (5, 1), (4, 1), (2, 3), (0, 2), (1, 2), (0, 3), (4, 2), (3, 1), (1, 3), (5, 2), (4, 3), (3, 2), (5, 3), (3, 3))
WT = 512
COEFF = math.sqrt(2.0 / math.pi)


def gelu_and_slope(value):
    square = value * value
    tangent = jnp.tanh(COEFF * value * (1.0 + 0.044715 * square))
    gelu = 0.5 * value * (1.0 + tangent)
    slope = 0.5 * (1.0 + tangent) + 0.5 * value * (1.0 - tangent * tangent) * COEFF * (
        1.0 + 3.0 * 0.044715 * square
    )
    return gelu, slope


LANES = dict(z=(20.2, 2.0), y=(20.2, 2.6), x=(20.2, 2.6), core=(4.0, 2.0))


class Move:
    def __init__(self, copy, lane, src, hops=1):
        self.dma, self.lane, self.landed = copy, lane, None
        rate, self.lag = LANES[lane.rstrip("+-")]
        self.busy = rate * math.prod(src.shape) * 2e-6 * hops
        self.lag += 0.6 * (hops - 1)


class Steps:
    def __init__(self):
        self.items = {}

    def add(self, key, rank, act=None, waits=(), starts=(), after=(), cost=0.0):
        self.items[key] = (rank, act, tuple(waits), tuple(starts), tuple(after), cost)

    def order(self):
        now, idle, left, done, out = 0.0, {}, dict(self.items), set(), []
        while left:
            best = None
            for key, (rank, _, waits, _, after, _) in left.items():
                if any(k not in done for k in after) or any(m.landed is None for m in waits):
                    continue
                ready = max([now] + [m.landed for m in waits])
                choice = (ready, rank, key)
                if best is None or choice[:2] < best[:2]:
                    best = choice
            ready, _, key = best
            _, _, _, starts, _, cost = left.pop(key)
            now = ready + cost
            for move in starts:
                now += 0.05
                begin = max(now, idle.get(move.lane, 0.0))
                idle[move.lane] = begin + move.busy
                move.landed = idle[move.lane] + move.lag
            done.add(key)
            out.append((ready, now, key))
        return out

    def emit(self):
        sent = []
        for _, _, key in self.order():
            _, act, waits, starts, _, _ = self.items[key]
            for move in waits:
                move.dma.wait_recv()
            if act is not None:
                act()
            for move in starts:
                move.dma.start()
                sent.append(move)
        for move in sent:
            move.dma.wait_send()


def kernel(
    gate, up, w, og, lout, ggrad, ugrad, dgrad,
    gv, uv, wv, hall, ogall, ogc, ogct, part, crecv, ysum, yhalf, yblk, hsend, hrecv, lov,
    gelu_s, us_s, ggv, guv, acc, losend, lorecv, own, gdv, sems,
):
    idx = {a: lax.axis_index(a) for a in AXES}
    z, lo, y, hi, c = (idx[a] for a in AXES)
    count = [0]

    def sem():
        count[0] += 1
        return sems.at[count[0] - 1]

    def shifted(axis, delta):
        return lax.rem(idx[axis] + (delta % SIZES[axis]), SIZES[axis])

    def at(axis, delta):
        return {axis: shifted(axis, delta)}

    def local(src, dst):
        return pltpu.make_async_copy(src, dst, sem())

    def remote(src, dst, axis, delta):
        copy = pltpu.make_async_remote_copy(
            src_ref=src, dst_ref=dst, send_sem=sem(), recv_sem=sem(),
            device_id=at(axis, delta), device_id_type=pl.DeviceIdType.MESH,
        )
        lane, hops = axis, 1
        if axis in ("hi", "lo"):
            lane = "x"
        elif axis in ("z", "y"):
            hops = min(delta, SIZES[axis] - delta)
            lane = axis + ("+" if delta == hops else "-")
        return Move(copy, lane, src, hops)

    peers = [("z", d) for d in range(1, 8)] + [("lo", 1), ("y", 1), ("y", 3), ("hi", 1), ("core", 1)]
    barrier = pltpu.get_barrier_semaphore()
    for axis, delta in peers:
        pl.semaphore_signal(
            barrier, inc=1, device_id=at(axis, delta), device_id_type=pl.DeviceIdType.MESH
        )

    def chunk_cols(k):
        return pl.ds(OFFSETS[k], WIDTHS[k])

    loads = []
    for k in range(len(WIDTHS)):
        pair = (
            local(gate.at[:, chunk_cols(k)], gv.at[:, chunk_cols(k)]),
            local(up.at[:, chunk_cols(k)], uv.at[:, chunk_cols(k)]),
        )
        loads.append(pair)

    def window(zt):
        return pl.ds(pl.multiple_of(lax.div(zt * 9, 2) * 128, 128), COLS)

    load_og = local(og, ogall.at[y, hi, c])
    load_ogc = local(og.at[:, window(z)], ogc.at[y, hi, c, 0])
    load_w = [
        local(w.at[:, pl.ds(j * WT, WT)], wv.at[:, pl.ds(j * WT, WT)]) for j in range(D // WT)
    ]
    for pair in loads[:1]:
        pair[0].start()
        pair[1].start()
    load_og.start()
    load_ogc.start()
    for pair in loads[1:]:
        pair[0].start()
        pair[1].start()
    for copy in load_w:
        copy.start()

    def hidden(k):
        loads[k][0].wait()
        loads[k][1].wait()
        cols = chunk_cols(k)
        up_value = uv[:, cols].astype(F32)
        gelu, slope = gelu_and_slope(gv[:, cols].astype(F32))
        hall[pl.ds(0, TOK), cols] = (gelu * up_value).astype(BF)
        gelu_s[:, cols] = gelu
        us_s[:, cols] = up_value * slope

    steps = Steps()
    add = steps.add
    chunks = range(len(WIDTHS))
    pl.semaphore_wait(barrier, len(peers))

    a2a = [
        remote(og.at[:, window(shifted("z", d))], ogc.at[y, hi, c, d], "z", d) for d in range(1, 8)
    ]
    add("columns out", 0, starts=a2a)

    def gather(name, buf, rank, act, waits, after, later):
        def move(yd, hd, axis, delta):
            ref = buf.at[shifted("y", yd), shifted("hi", hd), c]
            return remote(ref, ref, axis, delta)

        across = move(0, 0, "hi", 1)
        right = [move(0, 0, "y", 1), move(0, 1, "y", 1), move(3, 0, "y", 1)]
        left = [move(0, 0, "y", 3), move(0, 1, "y", 3), move(1, 1, "y", 3)]
        core = {(yd, hd): move(yd, hd, "core", 1) for yd in range(4) for hd in range(2)}

        def part(i, wait, *starts):
            add((name, i), rank, waits=(wait,), starts=starts, after=later.get(i, ()))

        add((name, 0), rank, act, waits, (right[0], left[0], across, core[0, 0]), after)
        part(1, across, right[1], left[1], core[0, 1])
        part(2, right[0], right[2], core[3, 0])
        part(3, left[0], core[1, 0])
        part(4, left[1], left[2], core[1, 1])
        part(5, right[1], core[3, 1])
        part(6, right[2], core[2, 0])
        part(7, left[2], core[2, 1])
        add((name, 8), rank, waits=core.values(), after=[(name, i) for i in range(8)])

    first_columns = {i: [("columns", 2), ("columns", 4)] for i in (2, 4)}
    gather("rows", ogall, 3, load_og.wait, (), ("columns out",), first_columns)
    gather("columns", ogc, 2, load_ogc.wait, a2a, (), {})

    hops = {}
    for k in chunks:
        cols = chunk_cols(k)
        for hop in range(4):
            first, size = 256 * hop, 256
            if hop == 3:
                size = 128
            hops[k, hop, 0] = remote(
                hall.at[pl.ds(first, size), cols], hall.at[pl.ds(first + 256, size), cols], "z", 1
            )
            first = 0 if hop == 0 else 256 * (8 - hop)
            into = 256 * (7 - hop)
            if hop == 3:
                first, into = first + 128, into + 128
            hops[k, hop, 1] = remote(
                hall.at[pl.ds(first, size), cols], hall.at[pl.ds(into, size), cols], "z", 7
            )
    for i, (k, hop) in enumerate(Z_ORDER):
        for way in range(2):
            after = [("z", *Z_ORDER[i - 1], way)] if i else ["columns out"]
            if hop == 0:
                after.append(("hidden", k))
            waits = (hops[k, hop - 1, way],) if hop else ()
            add(("z", k, hop, way), 1, waits=waits, starts=(hops[k, hop, way],), after=after)
    for k in chunks:
        add(
            ("hidden", k), 0 if k < 2 else 4, lambda k=k: hidden(k), cost=0.9 * WIDTHS[k] / 256,
            after=[("hidden", k - 1) if k else "columns out"],
        )

    def forward(j):
        load_w[j].wait()
        cols = pl.ds(j * WT, WT)
        out = jnp.dot(hall[pl.ds(0, TOK), :], wv[:, cols], preferred_element_type=F32)
        part[:, :, :, :, cols] = out.astype(BF).reshape(4, 2, 2, ROWS, WT)

    tiles = range(D // WT)
    for j in tiles:
        add(("forward", j), 5, lambda j=j: forward(j), after=[("hidden", k) for k in chunks], cost=0.6)

    core_send = {}
    for yd in (2, 1, 3, 0):
        yy = shifted("y", yd)
        core_send[yd] = remote(part.at[yy, :, 1 - c], crecv.at[yy], "core", 1)
    y2 = shifted("y", 2)
    half_send = [
        remote(ysum.at[y2, 0], yhalf.at[0], "y", 1),
        remote(ysum.at[y2, 1], yhalf.at[1], "y", 3),
    ]
    blk_send = [
        remote(ysum.at[shifted("y", 1)], yblk.at[0], "y", 1),
        remote(ysum.at[shifted("y", 3)], yblk.at[1], "y", 3),
    ]
    hi_send = remote(hsend, hrecv, "hi", 1)
    store_lout = local(lov, lout)

    def scatter_far():
        ysum[y2] = (part[y2, :, c].astype(F32) + crecv[y2].astype(F32)).astype(BF)

    def scatter_near(way):
        yy = shifted("y", 1 if way == 0 else 3)
        plain = 1 - way
        ysum[yy, plain] = (part[yy, plain, c].astype(F32) + crecv[yy, plain].astype(F32)).astype(BF)
        ysum[yy, way] = (
            part[yy, way, c].astype(F32) + crecv[yy, way].astype(F32) + yhalf[way].astype(F32)
        ).astype(BF)

    def mine(hh):
        total = part[y, hh, c].astype(F32) + crecv[y, hh].astype(F32)
        return total + yblk[0, hh].astype(F32) + yblk[1, hh].astype(F32)

    def scatter_hi():
        hsend[...] = mine(1 - hi).astype(BF)

    def scatter_end():
        lov[...] = (mine(hi) + hrecv[...].astype(F32)).astype(BF)
        store_lout.start()

    add("scatter core", 3, starts=core_send.values(), after=[("forward", j) for j in tiles])
    add("scatter far", 3, scatter_far, (core_send[2],), half_send, cost=0.3)
    for way in range(2):
        waits = (core_send[1 + 2 * way], half_send[way])
        add(("near", way), 3, lambda way=way: scatter_near(way), waits, (blk_send[way],), [("rows", 2), ("rows", 4)], cost=0.3)
    add("scatter hi", 3, scatter_hi, (core_send[0], *blk_send), (hi_send,), cost=0.2)
    add("scatter end", 3, scatter_end, (hi_send,), cost=0.2)

    stores = []

    def backward(k):
        cols = chunk_cols(k)
        group = ogall[...].reshape(TOK, D)
        grad = lax.dot_general(
            group, wv[cols, :], (((1,), (1,)), ((), ())), preferred_element_type=F32
        )
        ggv[:, cols] = (grad * us_s[:, cols]).astype(BF)
        guv[:, cols] = (grad * gelu_s[:, cols]).astype(BF)
        for src, dst in ((ggv, ggrad), (guv, ugrad)):
            copy = local(src.at[:, cols], dst.at[:, cols])
            copy.start()
            stores.append(copy)

    for k in chunks:
        add(("backward", k), 6, lambda k=k: backward(k), after=[("rows", 8)], cost=1.1 * WIDTHS[k] / 256)

    def transpose(s):
        block = ogc[:, :, :, s].reshape(TOK, COLS)
        ogct[:, pl.ds(TOK * s, TOK)] = block.T

    for s in range(8):
        add(("transpose", s), 2, lambda s=s: transpose(s), after=[("columns", 8)], cost=0.25)

    first_row = pl.multiple_of(64 * lax.rem(z, 2), 64)
    window_rows = pl.ds(first_row, 2 * OUT_COLS)
    lo_send = [
        remote(losend.at[:, chunk_cols(k)], lorecv.at[:, chunk_cols(k)], "lo", 1) for k in chunks
    ]

    def product(k, first, size):
        return jnp.dot(
            ogct[window_rows, pl.ds(first, size)], hall[pl.ds(first, size), chunk_cols(k)],
            preferred_element_type=F32,
        )

    def weight_most(k):
        acc[:, chunk_cols(k)] = product(k, 0, 1024) + product(k, 1280, 768)

    def weight_last(k):
        cols = chunk_cols(k)
        total = acc[:, cols] + product(k, 1024, 256)
        low, high = total[:OUT_COLS], total[OUT_COLS:]
        losend[:, cols] = jnp.where(lo == 0, high, low).astype(BF)
        own[:, cols] = jnp.where(lo == 0, low, high)

    def weight_end(k):
        cols = chunk_cols(k)
        gdv[:, cols] = (own[:, cols] + lorecv[:, cols].astype(F32)).astype(BF)
        copy = local(gdv.at[:, cols], dgrad.at[:, cols])
        copy.start()
        stores.append(copy)

    transposed = [("transpose", s) for s in range(8)]
    for k in chunks:
        after = transposed + [("z", k, 3, 0), ("z", k, 3, 1)]
        size = (WIDTHS[k] + 255) // 256
        add(("most", k), 2, lambda k=k: weight_most(k), after=after, cost=0.75 * size)
        add(
            ("last", k), 1, lambda k=k: weight_last(k), (hops[k, 3, 0], hops[k, 3, 1]),
            (lo_send[k],), [("most", k)], 0.3 * size,
        )
        add(("end", k), 3, lambda k=k: weight_end(k), (lo_send[k],), cost=0.2 * size)

    steps.emit()
    store_lout.wait()
    for copy in stores:
        copy.wait()


def body(gate, up, w, og):
    any_spec = pl.BlockSpec(memory_space=pl.ANY)
    shapes = (
        jax.ShapeDtypeStruct((ROWS, D), BF),
        jax.ShapeDtypeStruct((TOK, HB), BF),
        jax.ShapeDtypeStruct((TOK, HB), BF),
        jax.ShapeDtypeStruct((OUT_COLS, HB), BF),
    )
    v = pltpu.VMEM
    scratch = [
        v((TOK, HB), BF), v((TOK, HB), BF), v((HB, D), BF),
        v((8 * TOK, HB), BF), v((4, 2, 2, ROWS, D), BF), v((4, 2, 2, 8, ROWS, COLS), BF),
        v((COLS, 8 * TOK), BF),
        v((4, 2, 2, ROWS, D), BF), v((4, 2, ROWS, D), BF), v((4, 2, ROWS, D), BF),
        v((2, ROWS, D), BF), v((2, 2, ROWS, D), BF), v((ROWS, D), BF), v((ROWS, D), BF), v((ROWS, D), BF),
        v((TOK, HB), F32), v((TOK, HB), F32), v((TOK, HB), BF), v((TOK, HB), BF),
        v((2 * OUT_COLS, HB), F32),
        v((OUT_COLS, HB), BF), v((OUT_COLS, HB), BF), v((OUT_COLS, HB), F32), v((OUT_COLS, HB), BF),
        pltpu.SemaphoreType.DMA((256,)),
    ]
    results = pl.pallas_call(
        kernel,
        out_shape=shapes,
        in_specs=[any_spec] * 4,
        out_specs=(any_spec,) * 4,
        scratch_shapes=scratch,
        compiler_params=pltpu.CompilerParams(
            collective_id=0, has_side_effects=True, vmem_limit_bytes=60 * 2**20
        ),
        cost_estimate=pl.CostEstimate(
            flops=6 * TOK * HB * D, bytes_accessed=14_000_000, transcendentals=TOK * HB
        ),
        name="geglu_down",
    )(gate, up, w, og)
    layer_out, grad_gate, grad_up, grad_down = finish(results)
    return layer_out, grad_gate, grad_up, grad_down.T


def finish_kernel(*refs):
    n = len(refs) // 3
    sources, targets, held = refs[:n], refs[n : 2 * n], refs[2 * n : 3 * n]
    sems = refs[3 * n]
    moves = []
    for source, target, mid in zip(sources, targets, held):
        rows = source.shape[0]
        pieces = 1 if rows < 128 else 4 if rows % 64 == 0 else 3
        for piece in range(pieces):
            part = pl.ds(piece * (rows // pieces), rows // pieces)
            k = len(moves)
            moves.append(
                (
                    pltpu.make_async_copy(source.at[part], mid.at[part], sems.at[0, k]),
                    pltpu.make_async_copy(mid.at[part], target.at[part], sems.at[1, k]),
                )
            )
    for first, _ in moves:
        first.start()
    for first, second in moves:
        first.wait()
        second.start()
    for _, second in moves:
        second.wait()


def finish(results):
    any_spec = pl.BlockSpec(memory_space=pl.ANY)
    n = len(results)
    return pl.pallas_call(
        finish_kernel,
        out_shape=tuple(jax.ShapeDtypeStruct(r.shape, r.dtype) for r in results),
        in_specs=[any_spec] * n,
        out_specs=(any_spec,) * n,
        scratch_shapes=[pltpu.VMEM(r.shape, r.dtype) for r in results]
        + [pltpu.SemaphoreType.DMA((2, 4 * n))],
        compiler_params=pltpu.CompilerParams(vmem_limit_bytes=60 * 2**20),
        name="finish",
    )(*results)


def solution(mesh):
    fine = Mesh(mesh.devices.reshape(tuple(SIZES[a] for a in AXES)), AXES)
    dp, tensor = ("z", "lo"), ("y", "hi", "core")
    return jax.shard_map(
        body,
        mesh=fine,
        in_specs=(P(dp, tensor), P(dp, tensor), P(tensor, None), P(dp + tensor, None)),
        out_specs=(P(dp + tensor, None), P(dp, tensor), P(dp, tensor), P(tensor, dp)),
        check_vma=False,
    )
```

```python
import math

import jax
import jax.numpy as jnp
from jax import lax
from jax.experimental import pallas as pl
from jax.experimental.pallas import tpu as pltpu
from jax.sharding import Mesh, PartitionSpec as P

BF = jnp.bfloat16
F32 = jnp.float32
AXES = ("z", "lo", "y", "hi", "core")
SIZES = dict(z=8, lo=2, y=4, hi=2, core=2)
D, HB, TOK, ROWS = 4608, 1152, 256, 16
COLS = 640
OUT_COLS = 288
WIDTHS = (256, 256, 256, 128, 128, 128)
OFFSETS = tuple(sum(WIDTHS[:i]) for i in range(len(WIDTHS)))
Z_ORDER = ((3, 0), (2, 0), (1, 0), (0, 0), (2, 1), (0, 1), (1, 1), (5, 0), (4, 0), (2, 2), (5, 1), (4, 1), (2, 3), (0, 2), (1, 2), (0, 3), (4, 2), (3, 1), (1, 3), (5, 2), (4, 3), (3, 2), (5, 3), (3, 3))
WT = 512
COEFF = math.sqrt(2.0 / math.pi)


def gelu_and_slope(value):
    square = value * value
    tangent = jnp.tanh(COEFF * value * (1.0 + 0.044715 * square))
    gelu = 0.5 * value * (1.0 + tangent)
    slope = 0.5 * (1.0 + tangent) + 0.5 * value * (1.0 - tangent * tangent) * COEFF * (
        1.0 + 3.0 * 0.044715 * square
    )
    return gelu, slope


LANES = dict(z=(20.2, 2.0), y=(20.2, 2.6), x=(20.2, 2.6), core=(4.0, 2.0))


class Move:
    def __init__(self, copy, lane, src, hops=1):
        self.dma, self.lane, self.landed = copy, lane, None
        rate, self.lag = LANES[lane.rstrip("+-")]
        self.busy = rate * math.prod(src.shape) * 2e-6 * hops
        self.lag += 0.6 * (hops - 1)


class Steps:
    def __init__(self):
        self.items = {}

    def add(self, key, rank, act=None, waits=(), starts=(), after=(), cost=0.0):
        self.items[key] = (rank, act, tuple(waits), tuple(starts), tuple(after), cost)

    def order(self):
        now, idle, left, done, out = 0.0, {}, dict(self.items), set(), []
        while left:
            best = None
            for key, (rank, _, waits, _, after, _) in left.items():
                if any(k not in done for k in after) or any(m.landed is None for m in waits):
                    continue
                ready = max([now] + [m.landed for m in waits])
                choice = (ready, rank, key)
                if best is None or choice[:2] < best[:2]:
                    best = choice
            ready, _, key = best
            _, _, _, starts, _, cost = left.pop(key)
            now = ready + cost
            for move in starts:
                now += 0.05
                begin = max(now, idle.get(move.lane, 0.0))
                idle[move.lane] = begin + move.busy
                move.landed = idle[move.lane] + move.lag
            done.add(key)
            out.append((ready, now, key))
        return out

    def emit(self):
        sent = []
        for _, _, key in self.order():
            _, act, waits, starts, _, _ = self.items[key]
            for move in waits:
                move.dma.wait_recv()
            if act is not None:
                act()
            for move in starts:
                move.dma.start()
                sent.append(move)
        for move in sent:
            move.dma.wait_send()


def kernel(
    gate, up, w, og, lov, ggv, guv, gdv,
    gv, uv, wv, hall, ogall, ogc, ogct, part, crecv, ysum, yhalf, yblk, hsend, hrecv,
    gelu_s, us_s, acc, losend, lorecv, own, sems,
):
    idx = {a: lax.axis_index(a) for a in AXES}
    z, lo, y, hi, c = (idx[a] for a in AXES)
    count = [0]

    def sem():
        count[0] += 1
        return sems.at[count[0] - 1]

    def shifted(axis, delta):
        return lax.rem(idx[axis] + (delta % SIZES[axis]), SIZES[axis])

    def at(axis, delta):
        return {axis: shifted(axis, delta)}

    def local(src, dst):
        return pltpu.make_async_copy(src, dst, sem())

    def remote(src, dst, axis, delta):
        copy = pltpu.make_async_remote_copy(
            src_ref=src, dst_ref=dst, send_sem=sem(), recv_sem=sem(),
            device_id=at(axis, delta), device_id_type=pl.DeviceIdType.MESH,
        )
        lane, hops = axis, 1
        if axis in ("hi", "lo"):
            lane = "x"
        elif axis in ("z", "y"):
            hops = min(delta, SIZES[axis] - delta)
            lane = axis + ("+" if delta == hops else "-")
        return Move(copy, lane, src, hops)

    peers = [("z", d) for d in range(1, 8)] + [("lo", 1), ("y", 1), ("y", 3), ("hi", 1), ("core", 1)]
    barrier = pltpu.get_barrier_semaphore()
    for axis, delta in peers:
        pl.semaphore_signal(
            barrier, inc=1, device_id=at(axis, delta), device_id_type=pl.DeviceIdType.MESH
        )

    def chunk_cols(k):
        return pl.ds(OFFSETS[k], WIDTHS[k])

    loads = []
    for k in range(len(WIDTHS)):
        pair = (
            local(gate.at[:, chunk_cols(k)], gv.at[:, chunk_cols(k)]),
            local(up.at[:, chunk_cols(k)], uv.at[:, chunk_cols(k)]),
        )
        loads.append(pair)

    def window(zt):
        return pl.ds(pl.multiple_of(lax.div(zt * 9, 2) * 128, 128), COLS)

    load_og = local(og, ogall.at[y, hi, c])
    load_ogc = local(og.at[:, window(z)], ogc.at[y, hi, c, 0])
    load_w = [
        local(w.at[:, pl.ds(j * WT, WT)], wv.at[:, pl.ds(j * WT, WT)]) for j in range(D // WT)
    ]
    for pair in loads[:1]:
        pair[0].start()
        pair[1].start()
    load_og.start()
    load_ogc.start()
    for pair in loads[1:]:
        pair[0].start()
        pair[1].start()
    for copy in load_w:
        copy.start()

    def hidden(k):
        loads[k][0].wait()
        loads[k][1].wait()
        cols = chunk_cols(k)
        up_value = uv[:, cols].astype(F32)
        gelu, slope = gelu_and_slope(gv[:, cols].astype(F32))
        hall[pl.ds(0, TOK), cols] = (gelu * up_value).astype(BF)
        gelu_s[:, cols] = gelu
        us_s[:, cols] = up_value * slope

    steps = Steps()
    add = steps.add
    chunks = range(len(WIDTHS))
    pl.semaphore_wait(barrier, len(peers))

    a2a = [
        remote(og.at[:, window(shifted("z", d))], ogc.at[y, hi, c, d], "z", d) for d in range(1, 8)
    ]
    add("columns out", 0, starts=a2a)

    def gather(name, buf, rank, act, waits, after, later):
        def move(yd, hd, axis, delta):
            ref = buf.at[shifted("y", yd), shifted("hi", hd), c]
            return remote(ref, ref, axis, delta)

        across = move(0, 0, "hi", 1)
        right = [move(0, 0, "y", 1), move(0, 1, "y", 1), move(3, 0, "y", 1)]
        left = [move(0, 0, "y", 3), move(0, 1, "y", 3), move(1, 1, "y", 3)]
        core = {(yd, hd): move(yd, hd, "core", 1) for yd in range(4) for hd in range(2)}

        def part(i, wait, *starts):
            add((name, i), rank, waits=(wait,), starts=starts, after=later.get(i, ()))

        add((name, 0), rank, act, waits, (right[0], left[0], across, core[0, 0]), after)
        part(1, across, right[1], left[1], core[0, 1])
        part(2, right[0], right[2], core[3, 0])
        part(3, left[0], core[1, 0])
        part(4, left[1], left[2], core[1, 1])
        part(5, right[1], core[3, 1])
        part(6, right[2], core[2, 0])
        part(7, left[2], core[2, 1])
        add((name, 8), rank, waits=core.values(), after=[(name, i) for i in range(8)])

    first_columns = {i: [("columns", 2), ("columns", 4)] for i in (2, 4)}
    gather("rows", ogall, 3, load_og.wait, (), ("columns out",), first_columns)
    gather("columns", ogc, 2, load_ogc.wait, a2a, (), {})

    hops = {}
    for k in chunks:
        cols = chunk_cols(k)
        for hop in range(4):
            first, size = 256 * hop, 256
            if hop == 3:
                size = 128
            hops[k, hop, 0] = remote(
                hall.at[pl.ds(first, size), cols], hall.at[pl.ds(first + 256, size), cols], "z", 1
            )
            first = 0 if hop == 0 else 256 * (8 - hop)
            into = 256 * (7 - hop)
            if hop == 3:
                first, into = first + 128, into + 128
            hops[k, hop, 1] = remote(
                hall.at[pl.ds(first, size), cols], hall.at[pl.ds(into, size), cols], "z", 7
            )
    for i, (k, hop) in enumerate(Z_ORDER):
        for way in range(2):
            after = [("z", *Z_ORDER[i - 1], way)] if i else ["columns out"]
            if hop == 0:
                after.append(("hidden", k))
            waits = (hops[k, hop - 1, way],) if hop else ()
            add(("z", k, hop, way), 1, waits=waits, starts=(hops[k, hop, way],), after=after)
    for k in chunks:
        add(
            ("hidden", k), 0 if k < 2 else 4, lambda k=k: hidden(k), cost=0.9 * WIDTHS[k] / 256,
            after=[("hidden", k - 1) if k else "columns out"],
        )

    def forward(j):
        load_w[j].wait()
        cols = pl.ds(j * WT, WT)
        out = jnp.dot(hall[pl.ds(0, TOK), :], wv[:, cols], preferred_element_type=F32)
        part[:, :, :, :, cols] = out.astype(BF).reshape(4, 2, 2, ROWS, WT)

    tiles = range(D // WT)
    for j in tiles:
        add(("forward", j), 5, lambda j=j: forward(j), after=[("hidden", k) for k in chunks], cost=0.6)

    core_send = {}
    for yd in (2, 1, 3, 0):
        yy = shifted("y", yd)
        core_send[yd] = remote(part.at[yy, :, 1 - c], crecv.at[yy], "core", 1)
    y2 = shifted("y", 2)
    half_send = [
        remote(ysum.at[y2, 0], yhalf.at[0], "y", 1),
        remote(ysum.at[y2, 1], yhalf.at[1], "y", 3),
    ]
    blk_send = [
        remote(ysum.at[shifted("y", 1)], yblk.at[0], "y", 1),
        remote(ysum.at[shifted("y", 3)], yblk.at[1], "y", 3),
    ]
    hi_send = remote(hsend, hrecv, "hi", 1)

    def scatter_far():
        ysum[y2] = (part[y2, :, c].astype(F32) + crecv[y2].astype(F32)).astype(BF)

    def scatter_near(way):
        yy = shifted("y", 1 if way == 0 else 3)
        plain = 1 - way
        ysum[yy, plain] = (part[yy, plain, c].astype(F32) + crecv[yy, plain].astype(F32)).astype(BF)
        ysum[yy, way] = (
            part[yy, way, c].astype(F32) + crecv[yy, way].astype(F32) + yhalf[way].astype(F32)
        ).astype(BF)

    def mine(hh):
        total = part[y, hh, c].astype(F32) + crecv[y, hh].astype(F32)
        return total + yblk[0, hh].astype(F32) + yblk[1, hh].astype(F32)

    def scatter_hi():
        hsend[...] = mine(1 - hi).astype(BF)

    def scatter_end():
        lov[...] = (mine(hi) + hrecv[...].astype(F32)).astype(BF)

    add("scatter core", 3, starts=core_send.values(), after=[("forward", j) for j in tiles])
    add("scatter far", 3, scatter_far, (core_send[2],), half_send, cost=0.3)
    for way in range(2):
        waits = (core_send[1 + 2 * way], half_send[way])
        add(("near", way), 3, lambda way=way: scatter_near(way), waits, (blk_send[way],), [("rows", 2), ("rows", 4)], cost=0.3)
    add("scatter hi", 3, scatter_hi, (core_send[0], *blk_send), (hi_send,), cost=0.2)
    add("scatter end", 3, scatter_end, (hi_send,), cost=0.2)

    def backward(k):
        cols = chunk_cols(k)
        group = ogall[...].reshape(TOK, D)
        grad = lax.dot_general(
            group, wv[cols, :], (((1,), (1,)), ((), ())), preferred_element_type=F32
        )
        ggv[:, cols] = (grad * us_s[:, cols]).astype(BF)
        guv[:, cols] = (grad * gelu_s[:, cols]).astype(BF)

    for k in chunks:
        add(("backward", k), 6, lambda k=k: backward(k), after=[("rows", 8)], cost=1.1 * WIDTHS[k] / 256)

    def transpose(s):
        block = ogc[:, :, :, s].reshape(TOK, COLS)
        ogct[:, pl.ds(TOK * s, TOK)] = block.T

    for s in range(8):
        add(("transpose", s), 2, lambda s=s: transpose(s), after=[("columns", 8)], cost=0.25)

    first_row = pl.multiple_of(64 * lax.rem(z, 2), 64)
    window_rows = pl.ds(first_row, 2 * OUT_COLS)
    lo_send = [
        remote(losend.at[:, chunk_cols(k)], lorecv.at[:, chunk_cols(k)], "lo", 1) for k in chunks
    ]

    def product(k, first, size):
        return jnp.dot(
            ogct[window_rows, pl.ds(first, size)], hall[pl.ds(first, size), chunk_cols(k)],
            preferred_element_type=F32,
        )

    def weight_most(k):
        acc[:, chunk_cols(k)] = product(k, 0, 1024) + product(k, 1280, 768)

    def weight_last(k):
        cols = chunk_cols(k)
        total = acc[:, cols] + product(k, 1024, 256)
        low, high = total[:OUT_COLS], total[OUT_COLS:]
        losend[:, cols] = jnp.where(lo == 0, high, low).astype(BF)
        own[:, cols] = jnp.where(lo == 0, low, high)

    def weight_end(k):
        cols = chunk_cols(k)
        gdv[:, cols] = (own[:, cols] + lorecv[:, cols].astype(F32)).astype(BF)

    transposed = [("transpose", s) for s in range(8)]
    for k in chunks:
        after = transposed + [("z", k, 3, 0), ("z", k, 3, 1)]
        size = (WIDTHS[k] + 255) // 256
        add(("most", k), 2, lambda k=k: weight_most(k), after=after, cost=0.75 * size)
        add(
            ("last", k), 1, lambda k=k: weight_last(k), (hops[k, 3, 0], hops[k, 3, 1]),
            (lo_send[k],), [("most", k)], 0.3 * size,
        )
        add(("end", k), 3, lambda k=k: weight_end(k), (lo_send[k],), cost=0.2 * size)

    steps.emit()


def body(gate, up, w, og):
    any_spec = pl.BlockSpec(memory_space=pl.ANY)
    v = pltpu.VMEM
    shapes = (v((ROWS, D), BF), v((TOK, HB), BF), v((TOK, HB), BF), v((OUT_COLS, HB), BF))
    scratch = [
        v((TOK, HB), BF), v((TOK, HB), BF), v((HB, D), BF),
        v((8 * TOK, HB), BF), v((4, 2, 2, ROWS, D), BF), v((4, 2, 2, 8, ROWS, COLS), BF),
        v((COLS, 8 * TOK), BF),
        v((4, 2, 2, ROWS, D), BF), v((4, 2, ROWS, D), BF), v((4, 2, ROWS, D), BF),
        v((2, ROWS, D), BF), v((2, 2, ROWS, D), BF), v((ROWS, D), BF), v((ROWS, D), BF),
        v((TOK, HB), F32), v((TOK, HB), F32),
        v((2 * OUT_COLS, HB), F32),
        v((OUT_COLS, HB), BF), v((OUT_COLS, HB), BF), v((OUT_COLS, HB), F32),
        pltpu.SemaphoreType.DMA((256,)),
    ]
    results = pl.pallas_call(
        kernel,
        out_shape=shapes,
        in_specs=[any_spec] * 4,
        out_specs=(pl.BlockSpec(memory_space=pltpu.VMEM),) * 4,
        scratch_shapes=scratch,
        compiler_params=pltpu.CompilerParams(
            collective_id=0, has_side_effects=True, vmem_limit_bytes=54 * 2**20
        ),
        cost_estimate=pl.CostEstimate(
            flops=6 * TOK * HB * D, bytes_accessed=14_000_000, transcendentals=TOK * HB
        ),
        name="geglu_down",
    )(gate, up, w, og)
    layer_out, grad_gate, grad_up, grad_down = finish(results)
    return layer_out, grad_gate, grad_up, grad_down.T


def finish_kernel(*refs):
    n = len(refs) // 2
    copies = []
    for source, target in zip(refs[:n], refs[n : 2 * n]):
        rows = source.shape[0]
        pieces = 1 if rows < 128 else 4 if rows % 64 == 0 else 3
        for piece in range(pieces):
            part = pl.ds(piece * (rows // pieces), rows // pieces)
            sem = refs[2 * n].at[len(copies)]
            copies.append(pltpu.make_async_copy(source.at[part], target.at[part], sem))
    for copy in copies:
        copy.start()
    for copy in copies:
        copy.wait()


def finish(results):
    n = len(results)
    return pl.pallas_call(
        finish_kernel,
        out_shape=tuple(jax.ShapeDtypeStruct(r.shape, r.dtype) for r in results),
        in_specs=[pl.BlockSpec(memory_space=pltpu.VMEM)] * n,
        out_specs=(pl.BlockSpec(memory_space=pl.ANY),) * n,
        scratch_shapes=[pltpu.SemaphoreType.DMA((4 * n,))],
        compiler_params=pltpu.CompilerParams(vmem_limit_bytes=16 * 2**20),
        name="finish",
    )(*results)


def solution(mesh):
    fine = Mesh(mesh.devices.reshape(tuple(SIZES[a] for a in AXES)), AXES)
    dp, tensor = ("z", "lo"), ("y", "hi", "core")
    return jax.shard_map(
        body,
        mesh=fine,
        in_specs=(P(dp, tensor), P(dp, tensor), P(tensor, None), P(dp + tensor, None)),
        out_specs=(P(dp + tensor, None), P(dp, tensor), P(dp, tensor), P(tensor, dp)),
        check_vma=False,
    )
```

```python
import math

import jax
import jax.numpy as jnp
from jax import lax
from jax.experimental import pallas as pl
from jax.experimental.pallas import tpu as pltpu
from jax.sharding import Mesh, PartitionSpec as P

BF = jnp.bfloat16
F32 = jnp.float32
AXES = ("z", "lo", "y", "hi", "core")
SIZES = dict(z=8, lo=2, y=4, hi=2, core=2)
D, HB, TOK, ROWS = 4608, 1152, 256, 16
COLS = 640
OUT_COLS = 288
WIDTHS = (256, 256, 256, 128, 128, 128)
OFFSETS = tuple(sum(WIDTHS[:i]) for i in range(len(WIDTHS)))
Z_ORDER = ((3, 0), (2, 0), (1, 0), (0, 0), (2, 1), (0, 1), (1, 1), (5, 0), (4, 0), (2, 2), (5, 1), (4, 1), (2, 3), (0, 2), (1, 2), (0, 3), (4, 2), (3, 1), (1, 3), (5, 2), (4, 3), (3, 2), (5, 3), (3, 3))
WT = 512
COEFF = math.sqrt(2.0 / math.pi)


def gelu_and_slope(value):
    square = value * value
    tangent = jnp.tanh(COEFF * value * (1.0 + 0.044715 * square))
    gelu = 0.5 * value * (1.0 + tangent)
    slope = 0.5 * (1.0 + tangent) + 0.5 * value * (1.0 - tangent * tangent) * COEFF * (
        1.0 + 3.0 * 0.044715 * square
    )
    return gelu, slope


LANES = dict(z=(19.4, 1.8), y=(20.2, 2.6), x=(20.2, 2.6), core=(4.0, 2.0))


class Move:
    def __init__(self, copy, lane, src, hops=1):
        self.dma, self.lane, self.landed = copy, lane, None
        rate, self.lag = LANES[lane.rstrip("+-")]
        self.busy = rate * math.prod(src.shape) * 2e-6 * hops
        self.lag += 0.6 * (hops - 1)


class Steps:
    def __init__(self):
        self.items = {}

    def add(self, key, rank, act=None, waits=(), starts=(), after=(), cost=0.0):
        self.items[key] = (rank, act, tuple(waits), tuple(starts), tuple(after), cost)

    def order(self):
        now, idle, left, done, out = 0.0, {}, dict(self.items), set(), []
        while left:
            best = None
            for key, (rank, _, waits, _, after, _) in left.items():
                if any(k not in done for k in after) or any(m.landed is None for m in waits):
                    continue
                ready = max([now] + [m.landed for m in waits])
                choice = (ready, rank, key)
                if best is None or choice[:2] < best[:2]:
                    best = choice
            ready, _, key = best
            _, _, _, starts, _, cost = left.pop(key)
            now = ready + cost
            for move in starts:
                now += 0.05
                begin = max(now, idle.get(move.lane, 0.0))
                idle[move.lane] = begin + move.busy
                move.landed = idle[move.lane] + move.lag
            done.add(key)
            out.append((ready, now, key))
        return out

    def emit(self):
        sent = []
        for _, _, key in self.order():
            _, act, waits, starts, _, _ = self.items[key]
            for move in waits:
                move.dma.wait_recv()
            if act is not None:
                act()
            for move in starts:
                move.dma.start()
                sent.append(move)
        for move in sent:
            move.dma.wait_send()


def kernel(
    gate, up, w, og, lov, ggv, guv, gdv,
    gv, uv, wv, hall, ogall, ogc, ogct, part, crecv, ysum, yhalf, yblk, hsend, hrecv,
    gelu_s, us_s, acc, losend, lorecv, own, sems,
):
    idx = {a: lax.axis_index(a) for a in AXES}
    z, lo, y, hi, c = (idx[a] for a in AXES)
    count = [0]

    def sem():
        count[0] += 1
        return sems.at[count[0] - 1]

    def shifted(axis, delta):
        return lax.rem(idx[axis] + (delta % SIZES[axis]), SIZES[axis])

    def at(axis, delta):
        return {axis: shifted(axis, delta)}

    def local(src, dst):
        return pltpu.make_async_copy(src, dst, sem())

    def remote(src, dst, axis, delta):
        copy = pltpu.make_async_remote_copy(
            src_ref=src, dst_ref=dst, send_sem=sem(), recv_sem=sem(),
            device_id=at(axis, delta), device_id_type=pl.DeviceIdType.MESH,
        )
        lane, hops = axis, 1
        if axis in ("hi", "lo"):
            lane = "x"
        elif axis in ("z", "y"):
            hops = min(delta, SIZES[axis] - delta)
            lane = axis + ("+" if delta == hops else "-")
        return Move(copy, lane, src, hops)

    peers = [("z", d) for d in range(1, 8)] + [("lo", 1), ("y", 1), ("y", 3), ("hi", 1), ("core", 1)]
    barrier = pltpu.get_barrier_semaphore()
    for axis, delta in peers:
        pl.semaphore_signal(
            barrier, inc=1, device_id=at(axis, delta), device_id_type=pl.DeviceIdType.MESH
        )

    def chunk_cols(k):
        return pl.ds(OFFSETS[k], WIDTHS[k])

    loads = []
    for k in range(len(WIDTHS)):
        pair = (
            local(gate.at[:, chunk_cols(k)], gv.at[:, chunk_cols(k)]),
            local(up.at[:, chunk_cols(k)], uv.at[:, chunk_cols(k)]),
        )
        loads.append(pair)

    def window(zt):
        return pl.ds(pl.multiple_of(lax.div(zt * 9, 2) * 128, 128), COLS)

    load_og = local(og, ogall.at[y, hi, c])
    load_ogc = local(og.at[:, window(z)], ogc.at[y, hi, c, 0])
    load_w = [
        local(w.at[:, pl.ds(j * WT, WT)], wv.at[:, pl.ds(j * WT, WT)]) for j in range(D // WT)
    ]
    order = [k for k, hop in Z_ORDER if hop == 0]
    for k in order[:1]:
        loads[k][0].start()
        loads[k][1].start()
    load_og.start()
    load_ogc.start()
    for k in order[1:]:
        loads[k][0].start()
        loads[k][1].start()
    for copy in load_w:
        copy.start()

    def hidden(k):
        loads[k][0].wait()
        loads[k][1].wait()
        cols = chunk_cols(k)
        up_value = uv[:, cols].astype(F32)
        gelu, slope = gelu_and_slope(gv[:, cols].astype(F32))
        hall[pl.ds(0, TOK), cols] = (gelu * up_value).astype(BF)
        gelu_s[:, cols] = gelu
        us_s[:, cols] = up_value * slope

    steps = Steps()
    add = steps.add
    chunks = range(len(WIDTHS))
    pl.semaphore_wait(barrier, len(peers))

    a2a = [
        remote(og.at[:, window(shifted("z", d))], ogc.at[y, hi, c, d], "z", d)
        for d in (4, 3, 5, 2, 6, 1, 7)
    ]
    add("columns out", 0, starts=a2a)

    def gather(name, buf, rank, act, waits, after, later):
        def move(yd, hd, axis, delta):
            ref = buf.at[shifted("y", yd), shifted("hi", hd), c]
            return remote(ref, ref, axis, delta)

        across = move(0, 0, "hi", 1)
        right = [move(0, 0, "y", 1), move(0, 1, "y", 1), move(3, 0, "y", 1)]
        left = [move(0, 0, "y", 3), move(0, 1, "y", 3), move(1, 1, "y", 3)]
        core = {(yd, hd): move(yd, hd, "core", 1) for yd in range(4) for hd in range(2)}

        def part(i, wait, *starts):
            add((name, i), rank, waits=(wait,), starts=starts, after=later.get(i, ()))

        add((name, 0), rank, act, waits, (right[0], left[0], across, core[0, 0]), after)
        part(1, across, right[1], left[1], core[0, 1])
        part(2, right[0], right[2], core[3, 0])
        part(3, left[0], core[1, 0])
        part(4, left[1], left[2], core[1, 1])
        part(5, right[1], core[3, 1])
        part(6, right[2], core[2, 0])
        part(7, left[2], core[2, 1])
        add((name, 8), rank, waits=core.values(), after=[(name, i) for i in range(8)])

    first_columns = {i: [("columns", 2), ("columns", 4)] for i in (2, 4)}
    gather("rows", ogall, 3, load_og.wait, (), ("columns out",), first_columns)
    gather("columns", ogc, 2, load_ogc.wait, a2a, (), {})

    hops = {}
    for k in chunks:
        cols = chunk_cols(k)
        for hop in range(4):
            first, size = 256 * hop, 256
            if hop == 3:
                size = 128
            hops[k, hop, 0] = remote(
                hall.at[pl.ds(first, size), cols], hall.at[pl.ds(first + 256, size), cols], "z", 1
            )
            first = 0 if hop == 0 else 256 * (8 - hop)
            into = 256 * (7 - hop)
            if hop == 3:
                first, into = first + 128, into + 128
            hops[k, hop, 1] = remote(
                hall.at[pl.ds(first, size), cols], hall.at[pl.ds(into, size), cols], "z", 7
            )
    for i, (k, hop) in enumerate(Z_ORDER):
        for way in range(2):
            after = [("z", *Z_ORDER[i - 1], way)] if i else ["columns out"]
            if hop == 0:
                after.append(("hidden", k))
            waits = (hops[k, hop - 1, way],) if hop else ()
            add(("z", k, hop, way), 1, waits=waits, starts=(hops[k, hop, way],), after=after)
    for i, k in enumerate(order):
        add(
            ("hidden", k), 0 if i < 3 else 4, lambda k=k: hidden(k), cost=0.9 * WIDTHS[k] / 256,
            after=[("hidden", order[i - 1]) if i else "columns out"],
        )

    def forward(j):
        load_w[j].wait()
        cols = pl.ds(j * WT, WT)
        out = jnp.dot(hall[pl.ds(0, TOK), :], wv[:, cols], preferred_element_type=F32)
        part[:, :, :, :, cols] = out.astype(BF).reshape(4, 2, 2, ROWS, WT)

    tiles = range(D // WT)
    for j in tiles:
        add(("forward", j), 5, lambda j=j: forward(j), after=[("hidden", k) for k in chunks], cost=0.6)

    core_send = {}
    for yd in (2, 1, 3, 0):
        yy = shifted("y", yd)
        core_send[yd] = remote(part.at[yy, :, 1 - c], crecv.at[yy], "core", 1)
    y2 = shifted("y", 2)
    half_send = [
        remote(ysum.at[y2, 0], yhalf.at[0], "y", 1),
        remote(ysum.at[y2, 1], yhalf.at[1], "y", 3),
    ]
    blk_send = [
        remote(ysum.at[shifted("y", 1)], yblk.at[0], "y", 1),
        remote(ysum.at[shifted("y", 3)], yblk.at[1], "y", 3),
    ]
    hi_send = remote(hsend, hrecv, "hi", 1)

    def scatter_far():
        ysum[y2] = (part[y2, :, c].astype(F32) + crecv[y2].astype(F32)).astype(BF)

    def scatter_near(way):
        yy = shifted("y", 1 if way == 0 else 3)
        plain = 1 - way
        ysum[yy, plain] = (part[yy, plain, c].astype(F32) + crecv[yy, plain].astype(F32)).astype(BF)
        ysum[yy, way] = (
            part[yy, way, c].astype(F32) + crecv[yy, way].astype(F32) + yhalf[way].astype(F32)
        ).astype(BF)

    def mine(hh):
        total = part[y, hh, c].astype(F32) + crecv[y, hh].astype(F32)
        return total + yblk[0, hh].astype(F32) + yblk[1, hh].astype(F32)

    def scatter_hi():
        hsend[...] = mine(1 - hi).astype(BF)

    def scatter_end():
        lov[...] = (mine(hi) + hrecv[...].astype(F32)).astype(BF)

    add("scatter core", 3, starts=core_send.values(), after=[("forward", j) for j in tiles])
    add("scatter far", 3, scatter_far, (core_send[2],), half_send, cost=0.3)
    for way in range(2):
        waits = (core_send[1 + 2 * way], half_send[way])
        add(("near", way), 3, lambda way=way: scatter_near(way), waits, (blk_send[way],), [("rows", 2), ("rows", 4)], cost=0.3)
    add("scatter hi", 3, scatter_hi, (core_send[0], *blk_send), (hi_send,), cost=0.2)
    add("scatter end", 3, scatter_end, (hi_send,), cost=0.2)

    def backward(k):
        cols = chunk_cols(k)
        group = ogall[...].reshape(TOK, D)
        grad = lax.dot_general(
            group, wv[cols, :], (((1,), (1,)), ((), ())), preferred_element_type=F32
        )
        ggv[:, cols] = (grad * us_s[:, cols]).astype(BF)
        guv[:, cols] = (grad * gelu_s[:, cols]).astype(BF)

    for k in chunks:
        add(("backward", k), 6, lambda k=k: backward(k), after=[("rows", 8)], cost=1.1 * WIDTHS[k] / 256)

    def transpose(s):
        block = ogc[:, :, :, s].reshape(TOK, COLS)
        ogct[:, pl.ds(TOK * s, TOK)] = block.T

    for s in range(8):
        add(("transpose", s), 2, lambda s=s: transpose(s), after=[("columns", 8)], cost=0.25)

    first_row = pl.multiple_of(64 * lax.rem(z, 2), 64)
    window_rows = pl.ds(first_row, 2 * OUT_COLS)
    lo_send = [
        remote(losend.at[:, chunk_cols(k)], lorecv.at[:, chunk_cols(k)], "lo", 1) for k in chunks
    ]

    def product(k, first, size):
        return jnp.dot(
            ogct[window_rows, pl.ds(first, size)], hall[pl.ds(first, size), chunk_cols(k)],
            preferred_element_type=F32,
        )

    def weight_most(k):
        acc[:, chunk_cols(k)] = product(k, 0, 1024) + product(k, 1280, 768)

    def weight_last(k):
        cols = chunk_cols(k)
        total = acc[:, cols] + product(k, 1024, 256)
        low, high = total[:OUT_COLS], total[OUT_COLS:]
        losend[:, cols] = jnp.where(lo == 0, high, low).astype(BF)
        own[:, cols] = jnp.where(lo == 0, low, high)

    def weight_end(k):
        cols = chunk_cols(k)
        gdv[:, cols] = (own[:, cols] + lorecv[:, cols].astype(F32)).astype(BF)

    transposed = [("transpose", s) for s in range(8)]
    for k in chunks:
        after = transposed + [("z", k, 3, 0), ("z", k, 3, 1)]
        size = (WIDTHS[k] + 255) // 256
        add(("most", k), 2, lambda k=k: weight_most(k), after=after, cost=0.75 * size)
        add(
            ("last", k), 1, lambda k=k: weight_last(k), (hops[k, 3, 0], hops[k, 3, 1]),
            (lo_send[k],), [("most", k)], 0.3 * size,
        )
        add(("end", k), 3, lambda k=k: weight_end(k), (lo_send[k],), cost=0.2 * size)

    steps.emit()


def body(gate, up, w, og):
    any_spec = pl.BlockSpec(memory_space=pl.ANY)
    v = pltpu.VMEM
    shapes = (v((ROWS, D), BF), v((TOK, HB), BF), v((TOK, HB), BF), v((OUT_COLS, HB), BF))
    scratch = [
        v((TOK, HB), BF), v((TOK, HB), BF), v((HB, D), BF),
        v((8 * TOK, HB), BF), v((4, 2, 2, ROWS, D), BF), v((4, 2, 2, 8, ROWS, COLS), BF),
        v((COLS, 8 * TOK), BF),
        v((4, 2, 2, ROWS, D), BF), v((4, 2, ROWS, D), BF), v((4, 2, ROWS, D), BF),
        v((2, ROWS, D), BF), v((2, 2, ROWS, D), BF), v((ROWS, D), BF), v((ROWS, D), BF),
        v((TOK, HB), F32), v((TOK, HB), F32),
        v((2 * OUT_COLS, HB), F32),
        v((OUT_COLS, HB), BF), v((OUT_COLS, HB), BF), v((OUT_COLS, HB), F32),
        pltpu.SemaphoreType.DMA((256,)),
    ]
    results = pl.pallas_call(
        kernel,
        out_shape=shapes,
        in_specs=[any_spec] * 4,
        out_specs=(pl.BlockSpec(memory_space=pltpu.VMEM),) * 4,
        scratch_shapes=scratch,
        compiler_params=pltpu.CompilerParams(
            collective_id=0, has_side_effects=True, vmem_limit_bytes=54 * 2**20
        ),
        cost_estimate=pl.CostEstimate(
            flops=6 * TOK * HB * D, bytes_accessed=14_000_000, transcendentals=TOK * HB
        ),
        name="geglu_down",
    )(gate, up, w, og)
    layer_out, grad_gate, grad_up, grad_down = finish(results)
    return layer_out, grad_gate, grad_up, grad_down.T


def finish_kernel(*refs):
    n = len(refs) // 2
    copies = []
    for source, target in zip(refs[:n], refs[n : 2 * n]):
        rows = source.shape[0]
        pieces = 1 if rows < 128 else 4 if rows % 64 == 0 else 3
        for piece in range(pieces):
            part = pl.ds(piece * (rows // pieces), rows // pieces)
            sem = refs[2 * n].at[len(copies)]
            copies.append(pltpu.make_async_copy(source.at[part], target.at[part], sem))
    for copy in copies:
        copy.start()
    for copy in copies:
        copy.wait()


def finish(results):
    n = len(results)
    return pl.pallas_call(
        finish_kernel,
        out_shape=tuple(jax.ShapeDtypeStruct(r.shape, r.dtype) for r in results),
        in_specs=[pl.BlockSpec(memory_space=pltpu.VMEM)] * n,
        out_specs=(pl.BlockSpec(memory_space=pl.ANY),) * n,
        scratch_shapes=[pltpu.SemaphoreType.DMA((4 * n,))],
        compiler_params=pltpu.CompilerParams(vmem_limit_bytes=16 * 2**20),
        name="finish",
    )(*results)


def solution(mesh):
    fine = Mesh(mesh.devices.reshape(tuple(SIZES[a] for a in AXES)), AXES)
    dp, tensor = ("z", "lo"), ("y", "hi", "core")
    return jax.shard_map(
        body,
        mesh=fine,
        in_specs=(P(dp, tensor), P(dp, tensor), P(tensor, None), P(dp + tensor, None)),
        out_specs=(P(dp + tensor, None), P(dp, tensor), P(dp, tensor), P(tensor, dp)),
        check_vma=False,
    )
```
